32 devices in a mesh: blk: 16 (over z, y, x), pipe: 2 (over core).
Axes of the slice: x: 2, y: 2, z: 4, core: 2. Of those that a mesh axis runs over, the one named last changes fastest.
Arguments:
- endpoints: bfloat16 [2, 2, 12, 2048, 128], P('pipe', None, None, 'blk'), may hold values from -6 to 6
- row_counts: int32 [2], replicated, may hold values from 1 to 12, as said below
- layer_order: int32 [4], replicated, may hold values from 0 to 3, each once
- depth_weight: float32 [4, 3, 3, 128], replicated, may hold values from -2 to 2
- point_weight: bfloat16 [4, 128, 128], replicated, may hold values from -0.5 to 0.5
- point_bias: float32 [4, 128], replicated, may hold values from -3 to 3
Outputs:
- endpoints_out: bfloat16 [2, 2, 12, 2048, 128], P('pipe', None, None, 'blk')
- grad_depth: float32 [4, 3, 3, 128], replicated
- grad_point: float32 [4, 128, 128], replicated
- grad_bias: float32 [4, 128], replicated
The draws below stay inside these ranges and needn't reach their ends.
Inputs may be any that keep to these rules, and one draw needn't show every extreme that they name: `row_counts`: one of the two counts is 12. `layer_order`: a permutation of the layers.
All inputs are finite; a program needn't handle non-finite values.
Results may differ from the reference program's by a relative error of at most 0.013.
Values may be sent and summed in bfloat16 or wider, within the bound.
No kernel may reach another device: no remote copies, remote signals or barrier semaphores. Data moves between devices by JAX's collectives and lax.ppermute only.
A program may use at most 64 MiB of HBM per device.

```python
import math
import jax
import jax.numpy as jnp
from jax import lax

C = 128
MICRO = 2
ROWS_MAX = 12
LAYERS = 4
ANGLES = 2048
N_PIPE = 2


def draw_row_counts(key, part):
    first_key, second_key = jax.random.split(jax.random.fold_in(key, 7))
    shorter = jax.random.randint(first_key, (), 1, ROWS_MAX)
    fullest = jax.random.randint(second_key, (), 0, MICRO)
    slots = jnp.arange(MICRO)
    return jnp.where(slots == fullest, ROWS_MAX, shorter).astype(jnp.int32)


def levels(stream_key, dims, cuts, low, largest):
    loudness, own = 1.0, jax.random.fold_in(stream_key, 6)
    for axis_at, shards_of in cuts:
        steps = jnp.exp(jax.random.uniform(jax.random.fold_in(own, axis_at), (shards_of,), jnp.float32, low / len(cuts), largest / len(cuts)))
        loudness = loudness * jnp.repeat(steps, dims[axis_at] // shards_of).reshape([-1 if axis == axis_at else 1 for axis in range(len(dims))])
    return loudness


def centred(key, extent, scale, limit, shards=(), dtype=jnp.bfloat16):
    result = scale * jax.random.normal(key, extent, jnp.float32)
    if shards:
        result = result * levels(key, extent, shards, -0.22, 0.18)
    return jnp.clip(result, -limit, limit).astype(dtype)


def setup_inputs(seed: int = 0) -> dict:
    seeds = jax.random.split(jax.random.key(seed), 7)
    return {
        "endpoints": centred(seeds[0], (N_PIPE, MICRO, ROWS_MAX, ANGLES, C), 1.0, 6.0, ((0, 2), (3, 16))),
        "row_counts": draw_row_counts(jax.random.fold_in(seeds[6], 71), 0),
        "layer_order": jax.random.permutation(seeds[2], LAYERS).astype(jnp.int32),
        "depth_weight": centred(seeds[3], (LAYERS, 3, 3, C), 9 ** -0.5, 2.0, (), jnp.float32),
        "point_weight": centred(seeds[4], (LAYERS, C, C), C ** -0.5, 0.5),
        "point_bias": centred(seeds[5], (LAYERS, C), 0.5, 3.0, (), jnp.float32),
    }


root_half = 0.7071067811865476
density_norm = 0.3989422804014327

def gelu_pair(preact):
    normal_cdf = 0.5 * (1.0 + lax.erf(preact * root_half))
    normal_pdf = density_norm * jnp.exp(-0.5 * preact * preact)
    return (preact * normal_cdf, normal_cdf + preact * normal_pdf)

def widen(activation):
    wrapped = jnp.concatenate([activation[:, -1:], activation, activation[:, :1]], axis=1)
    return jnp.pad(wrapped, ((1, 1), (0, 0), (0, 0)))

def mixing(padded, depth, point, offset_vec):
    height = padded.shape[0] - 2
    breadth = padded.shape[1] - 2
    channels = padded.shape[2]
    depthwise = jnp.zeros((height, breadth, channels), jnp.float32)
    for row_off in range(3):
        for col_off in range(3):
            depthwise = depthwise + depth[row_off, col_off] * padded[row_off:row_off + height, col_off:col_off + breadth].astype(jnp.float32)
    mixed_bf = depthwise.astype(jnp.bfloat16)
    preact = jnp.dot(mixed_bf.reshape(height * breadth, channels), point, preferred_element_type=jnp.float32)
    preact = preact.reshape(height, breadth, channels) + offset_vec
    return (mixed_bf, preact)

def retreat(cotangent, live_rows, depth, point, padded, mixed_bf, preact):
    height = padded.shape[0] - 2
    breadth = padded.shape[1] - 2
    channels = padded.shape[2]
    masked_grad = cotangent.astype(jnp.float32) * live_rows
    gated = (masked_grad * gelu_pair(preact)[1]).astype(jnp.bfloat16)
    flat_mix = mixed_bf.reshape(height * breadth, channels)
    flat_gate = gated.reshape(height * breadth, channels)
    point_term = lax.dot_general(flat_mix, flat_gate, (((0,), (0,)), ((), ())), preferred_element_type=jnp.float32)
    bias_term = lax.optimization_barrier(jnp.sum(gated.astype(jnp.float32), axis=(0, 1)))
    back_mix = lax.dot_general(flat_gate, point, (((1,), (1,)), ((), ())), preferred_element_type=jnp.float32)
    back_mix = back_mix.reshape(height, breadth, channels).astype(jnp.bfloat16)
    spread = widen(back_mix)
    back_float = back_mix.astype(jnp.float32)
    earlier = jnp.zeros((height, breadth, channels), jnp.float32)
    kernel_rows = []
    for row_off in range(3):
        kernel_row = []
        for col_off in range(3):
            kernel_row.append(lax.optimization_barrier(jnp.sum(back_float * padded[row_off:row_off + height, col_off:col_off + breadth].astype(jnp.float32), axis=(0, 1))))
            earlier = earlier + depth[row_off, col_off] * spread[2 - row_off:2 - row_off + height, 2 - col_off:2 - col_off + breadth].astype(jnp.float32)
        kernel_rows.append(jnp.stack(kernel_row))
    depth_term = jnp.stack(kernel_rows)
    previous = ((masked_grad + earlier) * live_rows).astype(jnp.bfloat16)
    return (previous, depth_term, point_term, bias_term)

def reference(endpoints, row_counts, layer_order, depth_weight, point_weight, point_bias):
    grad_depth = jnp.zeros(depth_weight.shape, jnp.float32)
    grad_point = jnp.zeros(point_weight.shape, jnp.float32)
    grad_bias = jnp.zeros(point_bias.shape, jnp.float32)
    outcomes = []
    input_grads = []
    for batch in range(MICRO):
        live_rows = (jnp.arange(ROWS_MAX)[:, None, None] < row_counts[batch]).astype(jnp.float32)
        activation = (endpoints[0, batch].astype(jnp.float32) * live_rows).astype(jnp.bfloat16)
        kept = []
        for position in range(LAYERS):
            layer_id = layer_order[position]
            depth = lax.dynamic_index_in_dim(depth_weight, layer_id, 0, keepdims=False)
            point = lax.dynamic_index_in_dim(point_weight, layer_id, 0, keepdims=False)
            offset_vec = lax.dynamic_index_in_dim(point_bias, layer_id, 0, keepdims=False)
            kept.append(activation)
            padded = widen(activation)
            mixed_bf, preact = mixing(padded, depth, point, offset_vec)
            activation = ((activation.astype(jnp.float32) + gelu_pair(preact)[0]) * live_rows).astype(jnp.bfloat16)
        outcomes.append(activation)
        cotangent = endpoints[1, batch]
        for position in range(LAYERS - 1, -1, -1):
            layer_id = layer_order[position]
            depth = lax.dynamic_index_in_dim(depth_weight, layer_id, 0, keepdims=False)
            point = lax.dynamic_index_in_dim(point_weight, layer_id, 0, keepdims=False)
            offset_vec = lax.dynamic_index_in_dim(point_bias, layer_id, 0, keepdims=False)
            padded = widen(kept[position])
            mixed_bf, preact = mixing(padded, depth, point, offset_vec)
            cotangent, depth_term, point_term, bias_term = retreat(cotangent, live_rows, depth, point, padded, mixed_bf, preact)
            grad_depth = grad_depth.at[layer_id].add(depth_term)
            grad_point = grad_point.at[layer_id].add(point_term)
            grad_bias = grad_bias.at[layer_id].add(bias_term)
        input_grads.append(cotangent)
    factor = 1.0 / math.sqrt(MICRO * ROWS_MAX * ANGLES)
    endpoints_out = jnp.stack([jnp.stack(input_grads), jnp.stack(outcomes)])
    return (endpoints_out, grad_depth * factor, grad_point * factor, grad_bias * factor)
```

```python
import functools
import math

import jax
import jax.numpy as jnp
from jax import lax
from jax.experimental import pallas as pl
from jax.experimental.pallas import tpu as pltpu
from jax.sharding import PartitionSpec as P

root_half = 0.7071067811865476
density_norm = 0.3989422804014327
bf16 = jnp.bfloat16
f32 = jnp.float32
LANES = 16
GRAD_ROWS = 144


def gelu_pair(preact):
    normal_cdf = 0.5 * (1.0 + lax.erf(preact * root_half))
    normal_pdf = density_norm * jnp.exp(-0.5 * preact * preact)
    return (preact * normal_cdf, normal_cdf + preact * normal_pdf)


def prepare_kernel(depth_ref, point_ref, forward_ref, backward_ref):
    layers = point_ref.shape[0]
    for layer in range(layers):
        point = point_ref[layer].astype(f32)
        flipped = point.T
        taps = depth_ref[layer]
        columns = jnp.concatenate([taps, jnp.zeros((7, taps.shape[1]), f32)], axis=0).T
        for tap in range(9):
            forward_ref[layer, tap] = (point * columns[:, tap : tap + 1]).astype(bf16)
            backward_ref[layer, 8 - tap] = (flipped * taps[tap : tap + 1]).astype(bf16)


def pair_weights(taps_ref, layer, channels):
    none = jnp.zeros((channels, channels), bf16)
    blocks = []
    for row in range(4):
        for col in range(3):
            upper = taps_ref[layer, row * 3 + col] if row < 3 else none
            lower = taps_ref[layer, (row - 1) * 3 + col] if row >= 1 else none
            blocks.append(jnp.concatenate([upper, lower], axis=1))
    return jnp.concatenate(blocks, axis=0)


def pair_product(grid_ref, weights, first, slabs):
    channels = grid_ref.shape[-1]
    pieces = [
        grid_ref[first + row, col : col + slabs].reshape(slabs * LANES, channels)
        for row in range(4)
        for col in range(3)
    ]
    return jnp.dot(jnp.concatenate(pieces, axis=1), weights, preferred_element_type=f32)


def put_row(grid_ref, row, values, slabs):
    channels = grid_ref.shape[-1]
    grid_ref[row + 1, 1 : slabs + 1] = values.astype(bf16).reshape(slabs, LANES, channels)
    head, tail = (values[:LANES], values[(slabs - 1) * LANES :])
    grid_ref[row + 1, 0] = pltpu.roll(tail, 1, 0).astype(bf16)
    grid_ref[row + 1, slabs + 1] = pltpu.roll(head, LANES - 1, 0).astype(bf16)


def window_kernel(
    counts_ref, order_ref, held_ref, swapped_ref, own_l, own_r, far_l, far_r,
    forward_ref, backward_ref, depth_ref, point_ref, bias_ref,
    kept_ref, sent_ref, grad_kept_ref, grad_sent_ref,
    stage, x0, x1, x2, x3, slopes, cotangent, gated, owned, totals, *, factor,
):
    height, breadth, channels = swapped_ref.shape
    margin = own_l.shape[1]
    width = breadth + 2 * margin
    slabs = width // LANES
    flat = slabs * LANES
    layers = point_ref.shape[0]
    half = layers // 2
    section = lax.axis_index("pipe")
    count = counts_ref[section]
    grids = (x0, x1, x2, x3)

    def load_row(row, left, middle, right):
        stage[row, 0:margin] = left.astype(f32)
        stage[row, margin : margin + breadth] = middle.astype(f32)
        stage[row, margin + breadth : width] = right.astype(f32)

    def regular(row):
        return jnp.concatenate(
            [stage[row, pl.ds(slab, LANES, stride=slabs)] for slab in range(slabs)], axis=0
        )

    def store_rows(target):
        for row in range(height):
            target[row] = stage[row, margin : margin + breadth].astype(bf16)

    def irregular(row, values):
        for slab in range(slabs):
            stage[row, pl.ds(slab, LANES, stride=slabs)] = values[slab * LANES : (slab + 1) * LANES]

    edge = jnp.zeros((slabs + 2, LANES, channels), bf16)
    for grid in grids + (gated,):
        grid[0] = edge
        grid[height + 1] = edge
    totals[...] = jnp.zeros(totals.shape, f32)

    @pl.when(section == 0)
    def _():
        for row in range(height):
            load_row(row, own_l[row], held_ref[0, 0, row], own_r[row])

    @pl.when(section != 0)
    def _():
        for row in range(height):
            load_row(row, far_l[row], swapped_ref[row], far_r[row])

    for row in range(height):
        live = (row < count).astype(f32)
        put_row(x0, row, regular(row) * live, slabs)

    @pl.when(section == 0)
    def _():
        for row in range(height):
            load_row(row, far_l[row], swapped_ref[row], far_r[row])

    @pl.when(section != 0)
    def _():
        for row in range(height):
            load_row(row, own_l[row], held_ref[0, 1, row], own_r[row])

    for row in range(height):
        cotangent[row] = regular(row)

    for position in range(layers):
        layer = order_ref[position]
        weights = pair_weights(forward_ref, layer, channels)
        offset = bias_ref[pl.ds(layer, 1)]
        for first in range(0, height, 2):
            preacts = pair_product(grids[position], weights, first, slabs)
            for step in range(2):
                row = first + step
                live = (row < count).astype(f32)
                preact = preacts[:, step * channels : (step + 1) * channels] + offset
                value, slope = gelu_pair(preact)
                before = grids[position][row + 1, 1 : slabs + 1].reshape(flat, channels)
                following = (before.astype(f32) + value) * live
                slopes[position, row] = slope * live
                if position + 1 < layers:
                    put_row(grids[position + 1], row, following, slabs)
                else:
                    irregular(row, following)

    @pl.when(section == 0)
    def _():
        store_rows(sent_ref)

    @pl.when(section != 0)
    def _():
        store_rows(kept_ref)

    lane = lax.broadcasted_iota(jnp.int32, (flat, 1), 0)
    angle = (lane % LANES) * slabs + lane // LANES
    within = ((angle >= margin) & (angle < margin + breadth)).astype(f32)

    for position in range(layers - 1, -1, -1):
        layer = order_ref[position]
        bias_sum = jnp.zeros((1, channels), f32)
        for row in range(height):
            value = cotangent[row] * slopes[position, row]
            put_row(gated, row, value, slabs)
            inside = value * within
            owned[row] = inside.astype(bf16)
            bias_sum = bias_sum + jnp.sum(inside, axis=0, keepdims=True)
        weights = pair_weights(backward_ref, layer, channels)
        for first in range(0, height, 2):
            spreads = pair_product(gated, weights, first, slabs)
            for step in range(2):
                row = first + step
                value = cotangent[row] + spreads[:, step * channels : (step + 1) * channels]
                if position > 0:
                    cotangent[row] = value
                else:
                    irregular(row, value * (row < count).astype(f32))
        upstream = owned[...].reshape(height * flat, channels)
        flipped = point_ref[layer].astype(f32).T
        point_sum = jnp.zeros((channels, channels), f32)
        for start in range(0, 9, 2):
            taps = range(start, min(start + 2, 9))
            shifted = jnp.concatenate(
                [
                    grids[position][tap // 3 : tap // 3 + height, tap % 3 : tap % 3 + slabs].reshape(
                        height * flat, channels
                    )
                    for tap in taps
                ],
                axis=1,
            )
            products = lax.dot_general(
                upstream, shifted, (((0,), (0,)), ((), ())), preferred_element_type=f32
            )
            for place, tap in enumerate(taps):
                product = products[:, place * channels : (place + 1) * channels]
                depth_row = depth_ref[layer, tap : tap + 1]
                point_sum = point_sum + product * depth_row
                totals[layer, channels + tap : channels + tap + 1] = factor * jnp.sum(
                    product * flipped, axis=0, keepdims=True
                )
        totals[layer, 0:channels] = factor * point_sum.T
        totals[layer, channels + 9 : channels + 10] = factor * bias_sum

    @pl.when(section == 0)
    def _():
        store_rows(kept_ref)

    @pl.when(section != 0)
    def _():
        store_rows(sent_ref)

    for layer in range(half):
        grad_kept_ref[layer] = totals[section * half + layer]
        grad_sent_ref[layer] = totals[(1 - section) * half + layer].astype(bf16)


def vmem(count):
    return [pl.BlockSpec(memory_space=pltpu.VMEM)] * count


def smem(count):
    return [pl.BlockSpec(memory_space=pltpu.SMEM)] * count


def partner_strides(size):
    groups, stride = ([], 1)
    while stride < size:
        if stride * 4 <= size:
            groups.append((stride, 2 * stride, 3 * stride))
            stride *= 4
        else:
            groups.append((stride,))
            stride *= 2
    return groups


def summed_over_blk(value):
    size = lax.axis_size("blk")
    for strides in partner_strides(size):
        mine = value.astype(bf16)
        others = [
            lax.ppermute(mine, "blk", [(i, i ^ stride) for i in range(size)]).astype(f32)
            for stride in strides
        ]
        value = mine.astype(f32) + others[0]
        if len(others) == 3:
            value = value + (others[1] + others[2])
    return value


def shards(endpoints, row_counts, layer_order, depth_weight, point_weight, point_bias):
    batches, height, breadth, channels = endpoints.shape[1:]
    layers = layer_order.shape[0]
    margin = 2 * layers
    size = lax.axis_size("blk")
    section = lax.axis_index("pipe")
    slabs = (breadth + 2 * margin) // LANES
    swap = [(0, 1), (1, 0)]
    other = 1 - section
    left_edges = endpoints[0, :, :, :margin]
    right_edges = endpoints[0, :, :, breadth - margin :]

    def at(value, place):
        return lax.dynamic_index_in_dim(value, place, 0, keepdims=False)

    def carried(value, step, cross):
        pairs = [
            (2 * i + p, 2 * ((i + step) % size) + (1 - p if cross else p))
            for i in range(size)
            for p in range(2)
        ]
        return lax.ppermute(value, ("blk", "pipe"), pairs)

    swapped = lax.ppermute(at(endpoints[0], other), "pipe", swap)
    own_l = carried(at(right_edges, section), 1, False)
    own_r = carried(at(left_edges, section), -1, False)
    far_l = carried(at(right_edges, other), 1, True)
    far_r = carried(at(left_edges, other), -1, True)

    depth_taps = depth_weight.reshape(layers, 9, channels)
    taps_shape = jax.ShapeDtypeStruct((layers, 9, channels, channels), bf16)
    forward_taps, backward_taps = pl.pallas_call(
        prepare_kernel,
        out_shape=[taps_shape, taps_shape],
        in_specs=vmem(2),
        out_specs=vmem(2),
        cost_estimate=pl.CostEstimate(flops=4000000, bytes_accessed=3000000, transcendentals=0),
        name="prepare",
    )(depth_taps, point_weight)

    factor = 1.0 / math.sqrt(batches * height * breadth * size)
    grid = pltpu.VMEM((height + 2, slabs + 2, LANES, channels), bf16)
    rows = pltpu.VMEM((height, slabs * LANES, channels), f32)
    half_shape = (layers // 2, GRAD_ROWS, channels)
    kept, sent, grad_kept, grad_sent = pl.pallas_call(
        functools.partial(window_kernel, factor=factor),
        out_shape=[
            jax.ShapeDtypeStruct((height, breadth, channels), bf16),
            jax.ShapeDtypeStruct((height, breadth, channels), bf16),
            jax.ShapeDtypeStruct(half_shape, f32),
            jax.ShapeDtypeStruct(half_shape, bf16),
        ],
        in_specs=smem(2) + vmem(11),
        out_specs=vmem(4),
        scratch_shapes=[
            pltpu.VMEM((height, breadth + 2 * margin, channels), f32),
            grid, grid, grid, grid,
            pltpu.VMEM((layers, height, slabs * LANES, channels), f32),
            rows,
            grid,
            pltpu.VMEM((height, slabs * LANES, channels), bf16),
            pltpu.VMEM((layers, GRAD_ROWS, channels), f32),
        ],
        compiler_params=pltpu.CompilerParams(vmem_limit_bytes=40 * 2**20),
        cost_estimate=pl.CostEstimate(
            flops=6 * layers * height * breadth * 9 * channels * channels,
            bytes_accessed=6000000,
            transcendentals=0,
        ),
        name="window",
    )(
        row_counts, layer_order, endpoints, swapped, own_l, own_r, far_l, far_r,
        forward_taps, backward_taps, depth_taps, point_weight, point_bias,
    )

    arrived = lax.ppermute(sent, "pipe", swap)
    result = jnp.where(section == 0, jnp.stack([kept, arrived]), jnp.stack([arrived, kept]))[None]

    mine = grad_kept + lax.ppermute(grad_sent, "pipe", swap).astype(f32)
    mine = summed_over_blk(mine)
    theirs = lax.ppermute(mine, "pipe", swap)
    summed = jnp.where(
        section == 0, jnp.concatenate([mine, theirs]), jnp.concatenate([theirs, mine])
    )
    return (
        result,
        summed[:, channels : channels + 9].reshape(layers, 3, 3, channels),
        summed[:, :channels],
        summed[:, channels + 9],
    )


def solution(mesh):
    in_specs = (P("pipe", None, None, "blk", None), P(), P(), P(), P(), P())
    out_specs = (P("pipe", None, None, "blk", None), P(), P(), P())
    return jax.shard_map(shards, mesh=mesh, in_specs=in_specs, out_specs=out_specs, check_vma=False)
```

```python
import functools
import math

import jax
import jax.numpy as jnp
from jax import lax
from jax.experimental import pallas as pl
from jax.experimental.pallas import tpu as pltpu
from jax.sharding import PartitionSpec as P

root_half = 0.7071067811865476
density_norm = 0.3989422804014327
bf16 = jnp.bfloat16
f32 = jnp.float32
LANES = 16
GRAD_ROWS = 144


def gelu_pair(preact):
    normal_cdf = 0.5 * (1.0 + lax.erf(preact * root_half))
    normal_pdf = density_norm * jnp.exp(-0.5 * preact * preact)
    return (preact * normal_cdf, normal_cdf + preact * normal_pdf)


def prepare_kernel(
    counts_hbm, order_hbm, depth_hbm, point_hbm, bias_hbm, endpoints_hbm,
    forward_ref, backward_ref, depth_ref, point_ref, bias_ref, mine_ref, other_ref, facts_ref,
    counts, order, sems,
):
    layers = point_ref.shape[0]
    section = lax.axis_index("pipe")
    copies = [
        pltpu.make_async_copy(source, target, sems.at[place])
        for place, (source, target) in enumerate(
            [
                (point_hbm, point_ref),
                (depth_hbm, depth_ref),
                (bias_hbm, bias_ref),
                (counts_hbm, counts),
                (order_hbm, order),
                (endpoints_hbm.at[0, 1 - section], other_ref),
                (endpoints_hbm.at[0, section], mine_ref),
            ]
        )
    ]
    for copy in copies:
        copy.start()
    copies[0].wait()
    copies[1].wait()
    for layer in range(layers):
        point = point_ref[layer].astype(f32)
        flipped = point.T
        taps = depth_ref[:, layer]
        columns = jnp.concatenate([taps, jnp.zeros((7, taps.shape[1]), f32)], axis=0).T
        for tap in range(9):
            forward_ref[layer, tap] = (point * columns[:, tap : tap + 1]).astype(bf16)
            backward_ref[layer, 8 - tap] = (flipped * taps[tap : tap + 1]).astype(bf16)
    for copy in copies[2:]:
        copy.wait()
    lane = lax.broadcasted_iota(jnp.int32, facts_ref.shape, 1)
    facts = jnp.where(lane == layers, counts[section], 0)
    for position in range(layers):
        facts = jnp.where(lane == position, order[position], facts)
    facts_ref[...] = facts


def pair_weights(taps_ref, layer, channels):
    none = jnp.zeros((channels, channels), bf16)
    blocks = []
    for row in range(4):
        for col in range(3):
            upper = taps_ref[layer, row * 3 + col] if row < 3 else none
            lower = taps_ref[layer, (row - 1) * 3 + col] if row >= 1 else none
            blocks.append(jnp.concatenate([upper, lower], axis=1))
    return jnp.concatenate(blocks, axis=0)


def pair_product(grid_ref, weights, first, slabs):
    channels = grid_ref.shape[-1]
    pieces = [
        grid_ref[first + row, col : col + slabs].reshape(slabs * LANES, channels)
        for row in range(4)
        for col in range(3)
    ]
    return jnp.dot(jnp.concatenate(pieces, axis=1), weights, preferred_element_type=f32)


def put_row(grid_ref, row, values, slabs):
    channels = grid_ref.shape[-1]
    grid_ref[row + 1, 1 : slabs + 1] = values.astype(bf16).reshape(slabs, LANES, channels)
    head, tail = (values[:LANES], values[(slabs - 1) * LANES :])
    grid_ref[row + 1, 0] = pltpu.roll(tail, 1, 0).astype(bf16)
    grid_ref[row + 1, slabs + 1] = pltpu.roll(head, LANES - 1, 0).astype(bf16)


def window_kernel(
    facts_ref, held_ref, swapped_ref, own_o, own_i, far_o, far_i,
    forward_ref, backward_ref, depth_ref, point_ref, bias_ref,
    kept_ref, sent_ref, grad_kept_ref, grad_sent_ref,
    stage, x0, x1, x2, x3, slopes, cotangent, gated, owned, totals, *, factor,
):
    height, breadth, channels = swapped_ref.shape
    margin = own_o.shape[2]
    width = breadth + 2 * margin
    slabs = width // LANES
    flat = slabs * LANES
    layers = point_ref.shape[0]
    half = layers // 2
    section = lax.axis_index("pipe")
    count = facts_ref[0, layers]
    grids = (x0, x1, x2, x3)

    odd = lax.axis_index("blk") % 2 == 1

    def load_row(row, outer, middle, inner):
        outer, inner = (outer.astype(f32), inner.astype(f32))
        stage[row, 0:margin] = jnp.where(odd, inner, outer)
        stage[row, margin : margin + breadth] = middle.astype(f32)
        stage[row, margin + breadth : width] = jnp.where(odd, outer, inner)

    def regular(row):
        return jnp.concatenate(
            [stage[row, pl.ds(slab, LANES, stride=slabs)] for slab in range(slabs)], axis=0
        )

    def store_rows(target):
        for row in range(height):
            target[row] = stage[row, margin : margin + breadth].astype(bf16)

    def irregular(row, values):
        for slab in range(slabs):
            stage[row, pl.ds(slab, LANES, stride=slabs)] = values[slab * LANES : (slab + 1) * LANES]

    edge = jnp.zeros((slabs + 2, LANES, channels), bf16)
    for grid in grids + (gated,):
        grid[0] = edge
        grid[height + 1] = edge
    totals[...] = jnp.zeros(totals.shape, f32)

    @pl.when(section == 0)
    def _():
        for row in range(height):
            load_row(row, own_o[0, row], held_ref[row], own_i[0, row])

    @pl.when(section != 0)
    def _():
        for row in range(height):
            load_row(row, far_o[1, row], swapped_ref[row], far_i[1, row])

    for row in range(height):
        live = (row < count).astype(f32)
        put_row(x0, row, regular(row) * live, slabs)

    @pl.when(section == 0)
    def _():
        for row in range(height):
            load_row(row, far_o[0, row], swapped_ref[row], far_i[0, row])

    @pl.when(section != 0)
    def _():
        for row in range(height):
            load_row(row, own_o[1, row], held_ref[row], own_i[1, row])

    for row in range(height):
        cotangent[row] = regular(row)

    for position in range(layers):
        layer = facts_ref[0, position]
        weights = pair_weights(forward_ref, layer, channels)
        offset = bias_ref[pl.ds(layer, 1)]
        for first in range(0, height, 2):
            preacts = pair_product(grids[position], weights, first, slabs)
            for step in range(2):
                row = first + step
                live = (row < count).astype(f32)
                preact = preacts[:, step * channels : (step + 1) * channels] + offset
                value, slope = gelu_pair(preact)
                before = grids[position][row + 1, 1 : slabs + 1].reshape(flat, channels)
                following = (before.astype(f32) + value) * live
                slopes[position, row] = slope * live
                if position + 1 < layers:
                    put_row(grids[position + 1], row, following, slabs)
                else:
                    irregular(row, following)

    @pl.when(section == 0)
    def _():
        store_rows(sent_ref)

    @pl.when(section != 0)
    def _():
        store_rows(kept_ref)

    lane = lax.broadcasted_iota(jnp.int32, (flat, 1), 0)
    angle = (lane % LANES) * slabs + lane // LANES
    within = ((angle >= margin) & (angle < margin + breadth)).astype(f32)

    for position in range(layers - 1, -1, -1):
        layer = facts_ref[0, position]
        bias_sum = jnp.zeros((1, channels), f32)
        for row in range(height):
            value = cotangent[row] * slopes[position, row]
            put_row(gated, row, value, slabs)
            inside = value * within
            owned[row] = inside.astype(bf16)
            bias_sum = bias_sum + jnp.sum(inside, axis=0, keepdims=True)
        weights = pair_weights(backward_ref, layer, channels)
        for first in range(0, height, 2):
            spreads = pair_product(gated, weights, first, slabs)
            for step in range(2):
                row = first + step
                value = cotangent[row] + spreads[:, step * channels : (step + 1) * channels]
                if position > 0:
                    cotangent[row] = value
                else:
                    irregular(row, value * (row < count).astype(f32))
        upstream = owned[...].reshape(height * flat, channels)
        flipped = point_ref[layer].astype(f32).T
        point_sum = jnp.zeros((channels, channels), f32)
        for start in range(0, 9, 2):
            taps = range(start, min(start + 2, 9))
            shifted = jnp.concatenate(
                [
                    grids[position][tap // 3 : tap // 3 + height, tap % 3 : tap % 3 + slabs].reshape(
                        height * flat, channels
                    )
                    for tap in taps
                ],
                axis=1,
            )
            products = lax.dot_general(
                upstream, shifted, (((0,), (0,)), ((), ())), preferred_element_type=f32
            )
            for place, tap in enumerate(taps):
                product = products[:, place * channels : (place + 1) * channels]
                depth_row = depth_ref[tap, pl.ds(layer, 1)]
                point_sum = point_sum + product * depth_row
                totals[layer, channels + tap : channels + tap + 1] = factor * jnp.sum(
                    product * flipped, axis=0, keepdims=True
                )
        totals[layer, 0:channels] = factor * point_sum.T
        totals[layer, channels + 9 : channels + 10] = factor * bias_sum

    @pl.when(section == 0)
    def _():
        store_rows(kept_ref)

    @pl.when(section != 0)
    def _():
        store_rows(sent_ref)

    for layer in range(half):
        grad_kept_ref[layer] = totals[section * half + layer]
        grad_sent_ref[layer] = totals[(1 - section) * half + layer].astype(bf16)


def unpack_kernel(
    kept_ref, arrived_ref, mine_ref, theirs_ref, result_hbm, depth_ref, point_ref, bias_ref, sems
):
    half, _, channels = mine_ref.shape
    section = lax.axis_index("pipe")
    kept_copy = pltpu.make_async_copy(kept_ref, result_hbm.at[0, section], sems.at[0])
    arrived_copy = pltpu.make_async_copy(arrived_ref, result_hbm.at[0, 1 - section], sems.at[1])
    kept_copy.start()
    arrived_copy.start()

    def place(source, layer):
        point_ref[layer] = source[0:channels]
        for tap in range(9):
            depth_ref[tap // 3, tap % 3, pl.ds(layer, 1)] = source[channels + tap : channels + tap + 1]
        bias_ref[pl.ds(layer, 1)] = source[channels + 9 : channels + 10]

    for layer in range(half):
        place(mine_ref.at[layer], section * half + layer)
        place(theirs_ref.at[layer], (1 - section) * half + layer)
    kept_copy.wait()
    arrived_copy.wait()


def vmem(count):
    return [pl.BlockSpec(memory_space=pltpu.VMEM)] * count


def smem(count):
    return [pl.BlockSpec(memory_space=pltpu.SMEM)] * count


def partner_strides(size):
    groups, stride = ([], 1)
    while stride < size:
        if stride * 4 <= size:
            groups.append((stride, 2 * stride, 3 * stride))
            stride *= 4
        else:
            groups.append((stride,))
            stride *= 2
    return groups


def summed_over_blk(value):
    size = lax.axis_size("blk")
    for strides in partner_strides(size):
        mine = value.astype(bf16)
        others = [
            lax.ppermute(mine, "blk", [(i, i ^ stride) for i in range(size)]).astype(f32)
            for stride in strides
        ]
        value = mine.astype(f32) + others[0]
        if len(others) == 3:
            value = value + (others[1] + others[2])
    return value


def shards(endpoints, row_counts, layer_order, depth_weight, point_weight, point_bias):
    batches, height, breadth, channels = endpoints.shape[1:]
    layers = layer_order.shape[0]
    margin = 2 * layers
    size = lax.axis_size("blk")
    section = lax.axis_index("pipe")
    slabs = (breadth + 2 * margin) // LANES
    swap = [(0, 1), (1, 0)]
    odd = lax.axis_index("blk") % 2
    far = breadth - margin
    pieces = [
        lax.dynamic_slice(
            endpoints[0], (0, 0, start, 0), (batches, height, margin, channels)
        )
        for start in (odd * far, (1 - odd) * far)
    ]
    outward = [(i, (i + 1 if i % 2 else i - 1) % size) for i in range(size)]
    inward = [(i, i + 1 if i % 2 == 0 else i - 1) for i in range(size)]
    own_o = lax.ppermute(pieces[0], "blk", outward)
    own_i = lax.ppermute(pieces[1], "blk", inward)

    depth_taps = depth_weight.transpose(1, 2, 0, 3).reshape(9, layers, channels)
    taps_shape = jax.ShapeDtypeStruct((layers, 9, channels, channels), bf16)
    grid_shape = jax.ShapeDtypeStruct((height, breadth, channels), bf16)
    prepared = pl.pallas_call(
        prepare_kernel,
        out_shape=[
            taps_shape,
            taps_shape,
            jax.ShapeDtypeStruct(depth_taps.shape, f32),
            jax.ShapeDtypeStruct(point_weight.shape, bf16),
            jax.ShapeDtypeStruct(point_bias.shape, f32),
            grid_shape,
            grid_shape,
            jax.ShapeDtypeStruct((8, channels), jnp.int32),
        ],
        in_specs=[pl.BlockSpec(memory_space=pltpu.HBM)] * 6,
        out_specs=vmem(8),
        scratch_shapes=[
            pltpu.SMEM(row_counts.shape, jnp.int32),
            pltpu.SMEM(layer_order.shape, jnp.int32),
            pltpu.SemaphoreType.DMA((7,)),
        ],
        compiler_params=pltpu.CompilerParams(vmem_limit_bytes=8 * 2**20),
        cost_estimate=pl.CostEstimate(flops=4000000, bytes_accessed=4000000, transcendentals=0),
        name="prepare",
    )(
        *[
            pltpu.with_memory_space_constraint(value, pltpu.HBM)
            for value in (row_counts, layer_order, depth_taps, point_weight, point_bias, endpoints)
        ]
    )
    own_o, own_i, prepared = lax.optimization_barrier((own_o, own_i, prepared))
    forward_taps, backward_taps, depth_taps, points, biases, held, other, facts = prepared
    far_o = lax.ppermute(own_o, "pipe", swap)
    far_i = lax.ppermute(own_i, "pipe", swap)
    swapped = lax.ppermute(other, "pipe", swap)

    factor = 1.0 / math.sqrt(batches * height * breadth * size)
    grid = pltpu.VMEM((height + 2, slabs + 2, LANES, channels), bf16)
    rows = pltpu.VMEM((height, slabs * LANES, channels), f32)
    half_shape = (layers // 2, GRAD_ROWS, channels)
    kept, sent, grad_kept, grad_sent = pl.pallas_call(
        functools.partial(window_kernel, factor=factor),
        out_shape=[
            jax.ShapeDtypeStruct((height, breadth, channels), bf16),
            jax.ShapeDtypeStruct((height, breadth, channels), bf16),
            jax.ShapeDtypeStruct(half_shape, f32),
            jax.ShapeDtypeStruct(half_shape, bf16),
        ],
        in_specs=smem(1) + vmem(11),
        out_specs=vmem(4),
        scratch_shapes=[
            pltpu.VMEM((height, breadth + 2 * margin, channels), f32),
            grid, grid, grid, grid,
            pltpu.VMEM((layers, height, slabs * LANES, channels), f32),
            rows,
            grid,
            pltpu.VMEM((height, slabs * LANES, channels), bf16),
            pltpu.VMEM((layers, GRAD_ROWS, channels), f32),
        ],
        compiler_params=pltpu.CompilerParams(vmem_limit_bytes=40 * 2**20),
        cost_estimate=pl.CostEstimate(
            flops=6 * layers * height * breadth * 9 * channels * channels,
            bytes_accessed=6000000,
            transcendentals=0,
        ),
        name="window",
    )(
        facts, held, swapped, own_o, own_i, far_o, far_i,
        forward_taps, backward_taps, depth_taps, points, biases,
    )

    arrived = lax.ppermute(sent, "pipe", swap)
    mine = grad_kept + lax.ppermute(grad_sent, "pipe", swap).astype(f32)
    mine = summed_over_blk(mine)
    theirs = lax.ppermute(mine, "pipe", swap)
    result, grad_depth, grad_point, grad_bias = pl.pallas_call(
        unpack_kernel,
        out_shape=[
            jax.ShapeDtypeStruct(endpoints.shape, bf16),
            jax.ShapeDtypeStruct((3, 3, layers, channels), f32),
            jax.ShapeDtypeStruct((layers, channels, channels), f32),
            jax.ShapeDtypeStruct((layers, channels), f32),
        ],
        in_specs=vmem(4),
        out_specs=[pl.BlockSpec(memory_space=pltpu.HBM)] + vmem(3),
        scratch_shapes=[pltpu.SemaphoreType.DMA((2,))],
        compiler_params=pltpu.CompilerParams(vmem_limit_bytes=4 * 2**20),
        name="unpack",
    )(kept, arrived, mine, theirs)
    return (result, grad_depth.transpose(2, 0, 1, 3), grad_point, grad_bias)


def solution(mesh):
    in_specs = (P("pipe", None, None, "blk", None), P(), P(), P(), P(), P())
    out_specs = (P("pipe", None, None, "blk", None), P(), P(), P())
    return jax.shard_map(shards, mesh=mesh, in_specs=in_specs, out_specs=out_specs, check_vma=False)
```

```python
import functools
import math

import jax
import jax.numpy as jnp
from jax import lax
from jax.experimental import pallas as pl
from jax.experimental.pallas import tpu as pltpu
from jax.sharding import PartitionSpec as P

root_half = 0.7071067811865476
density_norm = 0.3989422804014327
bf16 = jnp.bfloat16
f32 = jnp.float32
LANES = 16
GRAD_ROWS = 144


def gelu_pair(preact):
    normal_cdf = 0.5 * (1.0 + lax.erf(preact * root_half))
    normal_pdf = density_norm * jnp.exp(-0.5 * preact * preact)
    return (preact * normal_cdf, normal_cdf + preact * normal_pdf)


def prepare_kernel(
    counts_hbm, order_hbm, depth_hbm, point_hbm, bias_hbm, endpoints_hbm,
    forward_ref, backward_ref, depth_ref, flipped_ref, bias_ref, mine_ref, facts_ref,
    counts, order, depth, point, bias, sems,
):
    layers = point.shape[0]
    section = lax.axis_index("pipe")
    copies = [
        pltpu.make_async_copy(source, target, sems.at[place])
        for place, (source, target) in enumerate(
            [
                (order_hbm, order),
                (point_hbm, point),
                (depth_hbm, depth),
                (bias_hbm, bias),
                (counts_hbm, counts),
                (endpoints_hbm.at[0, section], mine_ref),
            ]
        )
    ]
    for copy in copies:
        copy.start()
    for copy in copies[:3]:
        copy.wait()
    for position in range(layers):
        layer = order[position]
        weights = point[layer].astype(f32)
        flipped = weights.T
        flipped_ref[position] = flipped
        taps = jnp.concatenate([depth[tap, pl.ds(layer, 1)] for tap in range(9)], axis=0)
        depth_ref[position] = taps
        columns = jnp.concatenate([taps, jnp.zeros((7, taps.shape[1]), f32)], axis=0).T
        for tap in range(9):
            forward_ref[position, tap] = (weights * columns[:, tap : tap + 1]).astype(bf16)
            backward_ref[position, 8 - tap] = (flipped * taps[tap : tap + 1]).astype(bf16)
    for copy in copies[3:]:
        copy.wait()
    rows = []
    for position in range(layers):
        layer = order[position]
        bias_ref[position : position + 1] = bias[pl.ds(layer, 1)]
        rows.append(jnp.full((1, facts_ref.shape[1]), layer, jnp.int32))
    rows.append(jnp.full((1, facts_ref.shape[1]), counts[section], jnp.int32))
    facts_ref[...] = jnp.concatenate(rows, axis=0)


def pair_weights(taps_ref, layer, channels):
    none = jnp.zeros((channels, channels), bf16)
    blocks = []
    for row in range(4):
        for col in range(3):
            upper = taps_ref[layer, row * 3 + col] if row < 3 else none
            lower = taps_ref[layer, (row - 1) * 3 + col] if row >= 1 else none
            blocks.append(jnp.concatenate([upper, lower], axis=1))
    return jnp.concatenate(blocks, axis=0)


def pair_product(grid_ref, weights, first, slabs):
    channels = grid_ref.shape[-1]
    height = grid_ref.shape[0] - 2
    inner = range(1 if first == 0 else 0, 3 if first + 2 == height else 4)
    pieces = [
        grid_ref[first + row, col : col + slabs].reshape(slabs * LANES, channels)
        for row in inner
        for col in range(3)
    ]
    span = slice(3 * channels * inner.start, 3 * channels * inner.stop)
    return jnp.dot(jnp.concatenate(pieces, axis=1), weights[span], preferred_element_type=f32)


def put_row(grid_ref, row, values, slabs):
    channels = grid_ref.shape[-1]
    grid_ref[row + 1, 1 : slabs + 1] = values.astype(bf16).reshape(slabs, LANES, channels)
    head, tail = (values[:LANES], values[(slabs - 1) * LANES :])
    grid_ref[row + 1, 0] = pltpu.roll(tail, 1, 0).astype(bf16)
    grid_ref[row + 1, slabs + 1] = pltpu.roll(head, LANES - 1, 0).astype(bf16)


def weight_terms(position, grids, owned, bias_sums, depth_ref, flipped_ref, factor):
    height, flat, channels = owned.shape[1:]
    slabs = flat // LANES
    upstream = owned[position].reshape(height * flat, channels)
    flipped = flipped_ref[position]
    point_sum = jnp.zeros((channels, channels), f32)
    depth_rows = []
    for start in range(0, 9, 2):
        taps = range(start, min(start + 2, 9))
        shifted = jnp.concatenate(
            [
                grids[
                    position, tap // 3 : tap // 3 + height, tap % 3 : tap % 3 + slabs
                ].reshape(height * flat, channels)
                for tap in taps
            ],
            axis=1,
        )
        products = lax.dot_general(
            upstream, shifted, (((0,), (0,)), ((), ())), preferred_element_type=f32
        )
        for place, tap in enumerate(taps):
            product = products[:, place * channels : (place + 1) * channels]
            point_sum = point_sum + product * depth_ref[position, tap : tap + 1]
            depth_rows.append(factor * jnp.sum(product * flipped, axis=0, keepdims=True))
    rest = jnp.zeros((GRAD_ROWS - channels - 10, channels), f32)
    tail = jnp.concatenate(depth_rows + [factor * bias_sums[pl.ds(position, 1)], rest], axis=0)
    return (factor * point_sum.T, tail)


def irregular(stage, row, values, slabs):
    for slab in range(slabs):
        stage[row, pl.ds(slab, LANES, stride=slabs)] = values[slab * LANES : (slab + 1) * LANES]


def window_kernel(
    facts_ref, held_ref, swapped_ref, outer_ref, inner_ref,
    forward_ref, backward_ref, depth_ref, flipped_ref, bias_ref,
    grids, owned, bias_sums, gated, cotangent, final, terms_ref,
    stage, slopes, *, factor,
):
    height, breadth, channels = held_ref.shape
    margin = outer_ref.shape[2]
    width = breadth + 2 * margin
    slabs = width // LANES
    flat = slabs * LANES
    layers = flipped_ref.shape[0]
    half = layers // 2
    section = lax.axis_index("pipe")
    count = facts_ref[layers : layers + 1]
    odd = lax.axis_index("blk") % 2 == 1

    def load_row(row, outer, middle, inner):
        outer, inner = (outer.astype(f32), inner.astype(f32))
        stage[row, 0:margin] = jnp.where(odd, inner, outer)
        stage[row, margin : margin + breadth] = middle.astype(f32)
        stage[row, margin + breadth : width] = jnp.where(odd, outer, inner)

    def regular(row):
        return jnp.concatenate(
            [stage[row, pl.ds(slab, LANES, stride=slabs)] for slab in range(slabs)], axis=0
        )

    edge = jnp.zeros((slabs + 2, LANES, channels), bf16)
    for position in range(layers):
        grids[position, 0] = edge
        grids[position, height + 1] = edge
    gated[0] = edge
    gated[height + 1] = edge

    @pl.when(section == 0)
    def _():
        for row in range(height):
            load_row(row, outer_ref[0, row], held_ref[row], inner_ref[0, row])

    @pl.when(section != 0)
    def _():
        for row in range(height):
            load_row(row, outer_ref[1, row], swapped_ref[0, 1, row], inner_ref[1, row])

    for row in range(height):
        live = (row < count).astype(f32)
        put_row(grids.at[0], row, regular(row) * live, slabs)

    @pl.when(section == 0)
    def _():
        for row in range(height):
            load_row(row, outer_ref[1, row], swapped_ref[0, 0, row], inner_ref[1, row])

    @pl.when(section != 0)
    def _():
        for row in range(height):
            load_row(row, outer_ref[0, row], held_ref[row], inner_ref[0, row])

    for row in range(height):
        cotangent[row] = regular(row)

    for position in range(layers):
        weights = pair_weights(forward_ref, position, channels)
        offset = bias_ref[position : position + 1]
        for first in range(0, height, 2):
            preacts = pair_product(grids.at[position], weights, first, slabs)
            for step in range(2):
                row = first + step
                live = (row < count).astype(f32)
                preact = preacts[:, step * channels : (step + 1) * channels] + offset
                value, slope = gelu_pair(preact)
                before = grids[position, row + 1, 1 : slabs + 1].reshape(flat, channels)
                following = (before.astype(f32) + value) * live
                slopes[position, row] = slope * live
                if position + 1 < layers:
                    put_row(grids.at[position + 1], row, following, slabs)
                else:
                    irregular(final, row, following, slabs)

    lane = lax.broadcasted_iota(jnp.int32, (flat, 1), 0)
    angle = (lane % LANES) * slabs + lane // LANES
    within = ((angle >= margin) & (angle < margin + breadth)).astype(f32)

    for position in range(layers - 1, -1, -1):
        bias_sum = jnp.zeros((1, channels), f32)
        for row in range(height):
            value = cotangent[row] * slopes[position, row]
            put_row(gated, row, value, slabs)
            inside = value * within
            owned[position, row] = inside.astype(bf16)
            bias_sum = bias_sum + jnp.sum(inside, axis=0, keepdims=True)
        bias_sums[position : position + 1] = bias_sum
        if position > 0:
            weights = pair_weights(backward_ref, position, channels)
            for first in range(0, height, 2):
                spreads = pair_product(gated, weights, first, slabs)
                for step in range(2):
                    row = first + step
                    cotangent[row] = (
                        cotangent[row] + spreads[:, step * channels : (step + 1) * channels]
                    )

    for place in range(half):
        position = (1 - section) * half + place
        point_term, tail = weight_terms(
            position, grids, owned, bias_sums, depth_ref, flipped_ref, factor
        )
        terms_ref[place, 0:channels] = point_term.astype(bf16)
        terms_ref[place, channels:GRAD_ROWS] = tail.astype(bf16)


def kept_kernel(depth_ref, flipped_ref, grids, owned, bias_sums, terms_ref, *, factor):
    half, _, channels = terms_ref.shape
    section = lax.axis_index("pipe")
    for place in range(half):
        position = section * half + place
        point_term, tail = weight_terms(
            position, grids, owned, bias_sums, depth_ref, flipped_ref, factor
        )
        terms_ref[place, 0:channels] = point_term
        terms_ref[place, channels:GRAD_ROWS] = tail


def finish_kernel(
    facts_ref, backward_ref, gated, cotangent, final, kept_ref, sent_ref, stage
):
    height, breadth, channels = kept_ref.shape
    layers = backward_ref.shape[0]
    flat = cotangent.shape[1]
    slabs = flat // LANES
    margin = (flat - breadth) // 2
    section = lax.axis_index("pipe")
    count = facts_ref[layers : layers + 1]
    weights = pair_weights(backward_ref, 0, channels)
    for first in range(0, height, 2):
        spreads = pair_product(gated, weights, first, slabs)
        for step in range(2):
            row = first + step
            value = cotangent[row] + spreads[:, step * channels : (step + 1) * channels]
            irregular(stage, row, value * (row < count).astype(f32), slabs)

    def store(source, target):
        for row in range(height):
            target[row] = source[row, margin : margin + breadth].astype(bf16)

    @pl.when(section == 0)
    def _():
        store(stage, kept_ref)
        store(final, sent_ref)

    @pl.when(section != 0)
    def _():
        store(final, kept_ref)
        store(stage, sent_ref)


def deliver_kernel(kept_ref, arrived_ref, result_hbm, sems):
    section = lax.axis_index("pipe")
    kept_copy = pltpu.make_async_copy(kept_ref, result_hbm.at[0, section], sems.at[0])
    arrived_copy = pltpu.make_async_copy(arrived_ref, result_hbm.at[0, 1 - section], sems.at[1])
    kept_copy.start()
    arrived_copy.start()
    kept_copy.wait()
    arrived_copy.wait()


def unpack_kernel(facts_ref, mine_ref, theirs_ref, depth_ref, point_ref, bias_ref):
    half, _, channels = mine_ref.shape
    layers = 2 * half
    first = lax.axis_index("pipe") == 0

    for layer in range(layers):
        chosen = [facts_ref[position : position + 1] == layer for position in range(layers)]

        def pick(start, stop):
            result = jnp.zeros((stop - start, channels), f32)
            for slot in range(half):
                mine, theirs = (mine_ref[slot, start:stop], theirs_ref[slot, start:stop])
                early, late = (jnp.where(first, mine, theirs), jnp.where(first, theirs, mine))
                result = jnp.where(chosen[slot], early, result)
                result = jnp.where(chosen[half + slot], late, result)
            return result

        point_ref[layer] = pick(0, channels)
        rest = pick(channels, GRAD_ROWS)
        for tap in range(9):
            depth_ref[tap // 3, tap % 3, layer : layer + 1] = rest[tap : tap + 1]
        bias_ref[layer : layer + 1] = rest[9:10]


def vmem(count):
    return [pl.BlockSpec(memory_space=pltpu.VMEM)] * count


def partner_strides(size):
    groups, stride = ([], 1)
    while stride < size:
        if stride * 4 <= size:
            groups.append((stride, 2 * stride, 3 * stride))
            stride *= 4
        else:
            groups.append((stride,))
            stride *= 2
    return groups


def exchanged(value, strides):
    size = lax.axis_size("blk")
    mine = value.astype(bf16)
    return [mine] + [
        lax.ppermute(mine, "blk", [(i, i ^ stride) for i in range(size)]) for stride in strides
    ]


def added(parts):
    parts = [part.astype(f32) for part in parts]
    if len(parts) == 4:
        return (parts[0] + parts[1]) + (parts[2] + parts[3])
    return parts[0] + parts[1]


def shards(endpoints, row_counts, layer_order, depth_weight, point_weight, point_bias):
    batches, height, breadth, channels = endpoints.shape[1:]
    layers = layer_order.shape[0]
    margin = 2 * layers
    size = lax.axis_size("blk")
    section = lax.axis_index("pipe")
    slabs = (breadth + 2 * margin) // LANES
    swap = [(0, 1), (1, 0)]
    odd = lax.axis_index("blk") % 2
    far = breadth - margin
    edge_shape = (1, height, margin, channels)
    mine, other = [
        [
            lax.dynamic_slice(endpoints[0], (batch, 0, start, 0), edge_shape)
            for start in (odd * far, (1 - odd) * far)
        ]
        for batch in (section, 1 - section)
    ]
    got = lax.ppermute(jnp.concatenate(other), "pipe", swap)
    swapped = lax.ppermute(endpoints, "pipe", swap)
    outward = [(i, (i + 1 if i % 2 else i - 1) % size) for i in range(size)]
    inward = [(i, i + 1 if i % 2 == 0 else i - 1) for i in range(size)]
    outer = lax.ppermute(jnp.concatenate([mine[0], got[:1]]), "blk", outward)
    inner = lax.ppermute(jnp.concatenate([mine[1], got[1:]]), "blk", inward)

    depth_taps = depth_weight.transpose(1, 2, 0, 3).reshape(9, layers, channels)
    taps_shape = jax.ShapeDtypeStruct((layers, 9, channels, channels), bf16)
    grid_shape = jax.ShapeDtypeStruct((height, breadth, channels), bf16)
    prepared = pl.pallas_call(
        prepare_kernel,
        out_shape=[
            taps_shape,
            taps_shape,
            jax.ShapeDtypeStruct((layers, 9, channels), f32),
            jax.ShapeDtypeStruct(point_weight.shape, f32),
            jax.ShapeDtypeStruct(point_bias.shape, f32),
            grid_shape,
            jax.ShapeDtypeStruct((layers + 1, channels), jnp.int32),
        ],
        in_specs=[pl.BlockSpec(memory_space=pltpu.HBM)] * 6,
        out_specs=vmem(7),
        scratch_shapes=[
            pltpu.SMEM(row_counts.shape, jnp.int32),
            pltpu.SMEM(layer_order.shape, jnp.int32),
            pltpu.VMEM(depth_taps.shape, f32),
            pltpu.VMEM(point_weight.shape, bf16),
            pltpu.VMEM(point_bias.shape, f32),
            pltpu.SemaphoreType.DMA((6,)),
        ],
        compiler_params=pltpu.CompilerParams(vmem_limit_bytes=8 * 2**20),
        cost_estimate=pl.CostEstimate(flops=4000000, bytes_accessed=4000000, transcendentals=0),
        name="prepare",
    )(
        *[
            pltpu.with_memory_space_constraint(value, pltpu.HBM)
            for value in (row_counts, layer_order, depth_taps, point_weight, point_bias, endpoints)
        ]
    )
    forward_taps, backward_taps, depth_taps, flipped, biases, held, facts = prepared

    factor = 1.0 / math.sqrt(batches * height * breadth * size)
    half = layers // 2
    flat = slabs * LANES
    grid = (height + 2, slabs + 2, LANES, channels)
    rows = (height, flat, channels)
    terms = (half, GRAD_ROWS, channels)
    convolution = 2 * height * flat * 12 * channels * channels
    grids, owned, bias_sums, gated, cotangent, final, sent_terms = pl.pallas_call(
        functools.partial(window_kernel, factor=factor),
        out_shape=[
            jax.ShapeDtypeStruct((layers,) + grid, bf16),
            jax.ShapeDtypeStruct((layers,) + rows, bf16),
            jax.ShapeDtypeStruct((layers, channels), f32),
            jax.ShapeDtypeStruct(grid, bf16),
            jax.ShapeDtypeStruct(rows, f32),
            jax.ShapeDtypeStruct(rows, f32),
            jax.ShapeDtypeStruct(terms, bf16),
        ],
        in_specs=vmem(10),
        out_specs=vmem(7),
        scratch_shapes=[pltpu.VMEM(rows, f32), pltpu.VMEM((layers,) + rows, f32)],
        compiler_params=pltpu.CompilerParams(vmem_limit_bytes=16 * 2**20),
        cost_estimate=pl.CostEstimate(
            flops=10 * convolution, bytes_accessed=8000000, transcendentals=0
        ),
        name="window",
    )(
        facts, held, swapped, outer, inner,
        forward_taps, backward_taps, depth_taps, flipped, biases,
    )
    got_terms = lax.ppermute(sent_terms, "pipe", swap)
    kept_terms = pl.pallas_call(
        functools.partial(kept_kernel, factor=factor),
        out_shape=jax.ShapeDtypeStruct(terms, f32),
        in_specs=vmem(5),
        out_specs=pl.BlockSpec(memory_space=pltpu.VMEM),
        compiler_params=pltpu.CompilerParams(vmem_limit_bytes=8 * 2**20),
        cost_estimate=pl.CostEstimate(
            flops=2 * convolution, bytes_accessed=4000000, transcendentals=0
        ),
        name="kept_terms",
    )(depth_taps, flipped, grids, owned, bias_sums)
    kept, sent = pl.pallas_call(
        finish_kernel,
        out_shape=[grid_shape, grid_shape],
        in_specs=vmem(5),
        out_specs=vmem(2),
        scratch_shapes=[pltpu.VMEM(rows, f32)],
        compiler_params=pltpu.CompilerParams(vmem_limit_bytes=8 * 2**20),
        cost_estimate=pl.CostEstimate(
            flops=convolution, bytes_accessed=4000000, transcendentals=0
        ),
        name="finish",
    )(facts, backward_taps, gated, cotangent, final)

    total = kept_terms + got_terms.astype(f32)
    groups = partner_strides(size)
    for stage, strides in enumerate(groups):
        parts = exchanged(total, strides)
        if stage == 0:
            parts, kept, sent = lax.optimization_barrier((parts, kept, sent))
            arrived = lax.ppermute(sent, "pipe", swap)
        if stage + 1 == len(groups):
            result = pl.pallas_call(
                deliver_kernel,
                out_shape=jax.ShapeDtypeStruct(endpoints.shape, bf16),
                in_specs=vmem(2),
                out_specs=pl.BlockSpec(memory_space=pltpu.HBM),
                scratch_shapes=[pltpu.SemaphoreType.DMA((2,))],
                compiler_params=pltpu.CompilerParams(vmem_limit_bytes=2**20),
                cost_estimate=pl.CostEstimate(flops=0, bytes_accessed=3000000, transcendentals=0),
                name="deliver",
            )(kept, arrived)
            parts, result = lax.optimization_barrier((parts, result))
        total = added(parts)
    theirs = lax.ppermute(total, "pipe", swap)
    grad_depth, grad_point, grad_bias = pl.pallas_call(
        unpack_kernel,
        out_shape=[
            jax.ShapeDtypeStruct((3, 3, layers, channels), f32),
            jax.ShapeDtypeStruct((layers, channels, channels), f32),
            jax.ShapeDtypeStruct((layers, channels), f32),
        ],
        in_specs=vmem(3),
        out_specs=vmem(3),
        compiler_params=pltpu.CompilerParams(vmem_limit_bytes=4 * 2**20),
        name="unpack",
    )(facts, total, theirs)
    return (result, grad_depth.transpose(2, 0, 1, 3), grad_point, grad_bias)


def solution(mesh):
    in_specs = (P("pipe", None, None, "blk", None), P(), P(), P(), P(), P())
    out_specs = (P("pipe", None, None, "blk", None), P(), P(), P())
    return jax.shard_map(shards, mesh=mesh, in_specs=in_specs, out_specs=out_specs, check_vma=False)
```
